32 devices in a mesh: batch: 2 (over y), grp: 16 (over z, x, core).
Axes of the slice: x: 2, y: 2, z: 4, core: 2. Of those that a mesh axis runs over, the one named last changes fastest.
Arguments:
- amps: bfloat16 [6, 16, 1024, 128], P('batch', None, 'grp'), may hold values from -6 to 6
- cycle_inter: bfloat16 [6, 1024, 8, 128], P('batch', 'grp'), may hold values from -0.21875 to 0.21875
- k_irrep: int32 [6], replicated, may hold values from 0 to 7
- i_irrep: int32 [16], replicated, may hold values from 0 to 7
- j_irrep: int32 [8], replicated, may hold values from 0 to 7
- virt_count: int32 [8], replicated, may hold values from 64 to 128, as said below
Outputs:
- cycle_term: bfloat16 [16, 8, 1024, 128], P(None, 'batch', 'grp')
The draws below stay inside these ranges and needn't reach their ends.
Inputs may be any that keep to these rules, and one draw needn't show every extreme that they name: `virt_count`: together the counts are 800.
All inputs are finite; a program needn't handle non-finite values.
Results may differ from the reference program's by a relative error of at most 0.013.
Values may be sent and summed in bfloat16 or wider, within the bound.
No kernel may reach another device: no remote copies, remote signals or barrier semaphores. Data moves between devices by JAX's collectives and lax.ppermute only.
A program may use at most 64 MiB of HBM per device.

```python
import jax
import jax.numpy as jnp
from jax import lax

NIRREP = 8
SLOTS = 128
VS = 1024
OW = 16
J = 8
KB = 3
K = 6
N_BATCH = 2


def draw_virt_count(key, part):
    table = jnp.array([16, 8, 14, 11, 13, 12, 15, 11], jnp.int32) * (SLOTS // 16)
    order = jax.random.permutation(jax.random.fold_in(key, 11), 8)
    values = table[order]
    first = values[0::2]
    second = values[1::2]
    half = SLOTS // 2
    limit = jnp.minimum(jnp.minimum(SLOTS - first, first - half), jnp.minimum(SLOTS - second, second - half))
    shift = jax.random.randint(jax.random.fold_in(key, 23), (4,), -limit, limit + 1)
    paired = jnp.stack([first + shift, second - shift], axis=1)
    return paired.reshape(8).astype(jnp.int32)


def with_ends(values, key, least, top_value):
    extent = values.shape
    index_at = [jax.random.randint(jax.random.fold_in(key, axis), (), 0, extent[axis]) for axis in range(len(extent))]
    values = values.at[tuple(index_at)].set(least)
    longest = extent.index(max(extent))
    index_at[longest] = (index_at[longest] + 1) % extent[longest]
    return values.at[tuple(index_at)].set(top_value)


def shard_levels(rng, dims, split, least, largest):
    def one(dim, shards_of):
        steps = jax.random.uniform(jax.random.fold_in(jax.random.fold_in(rng, 6), dim), (shards_of,), jnp.float32, least / len(split), largest / len(split))
        return jnp.repeat(jnp.exp(steps), dims[dim] // shards_of).reshape((-1,) + (1,) * (len(dims) - dim - 1))

    gain = one(*split[0])
    for cut in split[1:]:
        gain = gain * one(*cut)
    return gain


def centred(rng, dims, deviation, reach, shards=(), held_as=jnp.bfloat16):
    values = jax.random.normal(rng, dims, jnp.float32) * deviation
    if len(shards) > 0:
        values = shard_levels(rng, dims, shards, -0.22, 0.18) * values
    return jnp.clip(values, min=-reach, max=reach).astype(held_as)


def setup_inputs(seed: int = 0) -> dict:
    splits = jax.random.split(jax.random.key(seed), 7)
    amps = centred(splits[0], (K, OW, VS, SLOTS), 1.0, 6.0, ((0, 2), (2, 16)))
    cycle_inter = centred(splits[1], (K, VS, J, SLOTS), (K * SLOTS) ** -0.5, 0.21875, ((0, 2), (1, 16)))
    k_irrep = with_ends(jax.random.randint(splits[2], (K,), 0, 8), jax.random.fold_in(splits[2], 1), 0, 7).astype(jnp.int32)
    i_irrep = with_ends(jax.random.randint(splits[3], (OW,), 0, 8), jax.random.fold_in(splits[3], 1), 0, 7).astype(jnp.int32)
    j_irrep = with_ends(jax.random.randint(splits[4], (J,), 0, 8), jax.random.fold_in(splits[4], 1), 0, 7).astype(jnp.int32)
    virt_count = draw_virt_count(jax.random.fold_in(splits[6], 71), 0)
    return dict(amps=amps, cycle_inter=cycle_inter, k_irrep=k_irrep, i_irrep=i_irrep, j_irrep=j_irrep, virt_count=virt_count)


def reference(amps, cycle_inter, k_irrep, i_irrep, j_irrep, virt_count):
    irreps = jnp.arange(NIRREP, dtype=jnp.int32)
    slot_pos = jnp.arange(SLOTS, dtype=jnp.int32)
    slot_index = jnp.arange(VS, dtype=jnp.int32)
    c_labels = slot_index // SLOTS
    c_live = (slot_index % SLOTS) < virt_count[c_labels]
    total = jnp.zeros((OW, J, VS, SLOTS), jnp.float32)
    for group in range(N_BATCH):
        partial_value = jnp.zeros((OW, J, NIRREP, SLOTS, SLOTS), jnp.float32)
        for local in range(KB):
            index = group * KB + local
            label = k_irrep[index]
            flip = jnp.bitwise_xor(label, i_irrep)
            a_labels = jnp.bitwise_xor(flip[:, None], c_labels[None, :])
            amp_mask = c_live[None, :, None] & (slot_pos[None, None, :] < virt_count[a_labels][:, :, None])
            amp_k = jnp.where(amp_mask, amps[index], jnp.zeros((), amps.dtype)).astype(jnp.float32)
            b_labels = jnp.bitwise_xor(jnp.bitwise_xor(label, c_labels)[:, None], j_irrep[None, :])
            inter_mask = c_live[:, None, None] & (slot_pos[None, None, :] < virt_count[b_labels][:, :, None])
            inter_k = jnp.where(inter_mask, cycle_inter[index], jnp.zeros((), cycle_inter.dtype)).astype(jnp.float32)
            products = jnp.einsum("inca,ncjb->ijnab", amp_k.reshape(OW, NIRREP, SLOTS, SLOTS), inter_k.reshape(NIRREP, SLOTS, J, SLOTS))
            source = jnp.bitwise_xor(irreps[None, :], flip[:, None]).astype(jnp.int32)
            partial_value = partial_value + jnp.take_along_axis(products, source[:, None, :, None, None], axis=2)
        rounded = lax.optimization_barrier(partial_value.reshape(OW, J, VS, SLOTS).astype(jnp.bfloat16))
        total = total + rounded.astype(jnp.float32)
    return total.astype(jnp.bfloat16)
```

```python
import functools

import jax
import jax.numpy as jnp
from jax import lax
from jax.experimental import pallas as pl
from jax.experimental.pallas import tpu as pltpu
from jax.sharding import PartitionSpec as P


def contract_kernel(n_k, width, labels_ref, *refs):
    amp_refs = refs[:n_k]
    inter_refs = refs[n_k:2 * n_k]
    out_ref = refs[2 * n_k]
    p = pl.program_id(0)
    n_irrep = pl.num_programs(0)
    j_count = out_ref.shape[1]
    i_label = labels_ref[n_k]
    j_first = n_k + 1
    count_first = j_first + j_count
    row = lax.broadcasted_iota(jnp.int32, (width, width), 0)
    col = lax.broadcasted_iota(jnp.int32, (width, width), 1)
    acc = None
    for k in range(n_k):
        c_count = labels_ref[count_first + (labels_ref[k] ^ i_label ^ p)]
        amp = amp_refs[k][...].reshape(width, width)
        amp = jnp.where(row < c_count, amp, jnp.zeros((), amp.dtype))
        inter = inter_refs[k][...].reshape(width, j_count * width)
        term = lax.dot_general(amp, inter, (((0,), (0,)), ((), ())), preferred_element_type=jnp.float32)
        acc = term if acc is None else acc + term
    a_count = labels_ref[count_first + p]
    parts, rows = out_ref.shape[0], out_ref.shape[2]
    for j in range(j_count):
        b_count = labels_ref[count_first + (p ^ i_label ^ labels_ref[j_first + j])]
        live = (row < a_count) & (col < b_count)
        block = jnp.where(live, acc[:, j * width:(j + 1) * width], 0.0).astype(out_ref.dtype)
        out_ref[:, j] = block.reshape(parts, rows, width)


def contract(labels, amps, inter, n_irrep, j_count):
    devices, _, slab, width = amps[0].shape
    parts = devices // n_irrep
    n_k = sum(x.shape[1] for x in amps)

    def block_of(k, at):
        def index(p, labels):
            return (labels[k] ^ labels[n_k] ^ p, at, 0, 0)
        return index

    amp_ops, amp_specs, inter_specs = [], [], []
    for a in amps:
        for at in range(a.shape[1]):
            amp_specs.append(pl.BlockSpec((parts, 1, slab, width), block_of(len(amp_ops), at)))
            amp_ops.append(a)
    for k in range(n_k):
        inter_specs.append(pl.BlockSpec((parts, 1, slab, j_count * width), block_of(k, k)))
    flops = 2 * n_k * n_irrep * width ** 3 * j_count
    return pl.pallas_call(
        functools.partial(contract_kernel, n_k, width),
        grid_spec=pltpu.PrefetchScalarGridSpec(
            num_scalar_prefetch=1,
            grid=(n_irrep,),
            in_specs=amp_specs + inter_specs,
            out_specs=pl.BlockSpec((parts, j_count, slab, width), lambda p, labels: (p, 0, 0, 0)),
        ),
        out_shape=jax.ShapeDtypeStruct((devices, j_count, slab, width), jnp.bfloat16),
        compiler_params=pltpu.CompilerParams(vmem_limit_bytes=48 * 2 ** 20),
        cost_estimate=pl.CostEstimate(flops=flops, bytes_accessed=flops // 128, transcendentals=0),
    )(labels, *amp_ops, *([inter] * n_k))


def shards(n_batch, n_grp, amps, cycle_inter, k_irrep, i_irrep, j_irrep, virt_count):
    k_local, i_total, slab, width = amps.shape
    n_irrep = virt_count.shape[0]
    j_total = cycle_inter.shape[2]
    j_count = j_total // n_batch
    me_b = lax.axis_index("batch")
    me_g = lax.axis_index("grp")
    i_count = i_total // n_grp

    split = cycle_inter.reshape(k_local, slab, n_batch, j_count * width)
    if n_batch == 2:
        swap = [(0, 1), (1, 0)]
        own = lax.dynamic_index_in_dim(split, me_b, 2, keepdims=False)
        away = lax.dynamic_index_in_dim(split, 1 - me_b, 2, keepdims=False)
        mine = jnp.concatenate([own, lax.ppermute(away, "batch", swap)])
        k_labels = jnp.concatenate([
            lax.dynamic_slice_in_dim(k_irrep, me_b * k_local, k_local),
            lax.dynamic_slice_in_dim(k_irrep, (1 - me_b) * k_local, k_local),
        ])
    else:
        mine = lax.all_to_all(split.transpose(2, 0, 1, 3), "batch", split_axis=0, concat_axis=0, tiled=True)
        mine = mine.reshape(n_batch * k_local, slab, j_count * width)
        k_labels = k_irrep
    inter_all = lax.all_gather(mine, "grp", axis=0, tiled=False)

    sends = amps.transpose(1, 0, 2, 3).reshape(n_grp, i_count, k_local, slab, width)
    got = lax.all_to_all(sends, "grp", split_axis=0, concat_axis=0, tiled=True)
    if n_batch == 2:
        amp_parts = [got, lax.ppermute(got, "batch", swap)]
    else:
        gathered = lax.all_gather(got, "batch", axis=0, tiled=False)
        amp_parts = [gathered[b] for b in range(n_batch)]

    j_labels = lax.dynamic_slice_in_dim(j_irrep, me_b * j_count, j_count)
    outs = []
    for i in range(i_count):
        i_label = lax.dynamic_slice_in_dim(i_irrep, me_g * i_count + i, 1)
        labels = jnp.concatenate([k_labels, i_label, j_labels, virt_count])
        outs.append(contract(labels, [a[:, i] for a in amp_parts], inter_all, n_irrep, j_count))
    partial = outs[0][:, None] if i_count == 1 else jnp.stack(outs, axis=1)
    result = lax.all_to_all(partial, "grp", split_axis=0, concat_axis=0, tiled=True)
    return result.reshape(i_total, j_count, slab, width)


def solution(mesh):
    return jax.shard_map(
        functools.partial(shards, mesh.shape["batch"], mesh.shape["grp"]),
        mesh=mesh,
        in_specs=(P("batch", None, "grp", None), P("batch", "grp", None, None), P(), P(), P(), P()),
        out_specs=P(None, "batch", "grp", None),
        check_vma=False,
    )
```

```python
import functools

import jax
import jax.numpy as jnp
from jax import lax
from jax.experimental import pallas as pl
from jax.experimental.pallas import tpu as pltpu
from jax.sharding import PartitionSpec as P


def contract_kernel(n_k, width, labels_ref, *refs):
    amp_refs = refs[:n_k]
    inter_refs = refs[n_k:2 * n_k]
    out_ref = refs[2 * n_k]
    p = pl.program_id(0)
    n_irrep = pl.num_programs(0)
    j_count = out_ref.shape[1]
    i_label = labels_ref[n_k]
    j_first = n_k + 1
    count_first = j_first + j_count
    row = lax.broadcasted_iota(jnp.int32, (width, width), 0)
    col = lax.broadcasted_iota(jnp.int32, (width, width), 1)
    acc = None
    for k in range(n_k):
        c_count = labels_ref[count_first + (labels_ref[k] ^ i_label ^ p)]
        amp = amp_refs[k][...].reshape(width, width)
        amp = jnp.where(row < c_count, amp, jnp.zeros((), amp.dtype))
        inter = inter_refs[k][...].reshape(width, j_count * width)
        term = lax.dot_general(amp, inter, (((0,), (0,)), ((), ())), preferred_element_type=jnp.float32)
        acc = term if acc is None else acc + term
    a_count = labels_ref[count_first + p]
    parts, rows = out_ref.shape[0], out_ref.shape[2]
    for j in range(j_count):
        b_count = labels_ref[count_first + (p ^ i_label ^ labels_ref[j_first + j])]
        live = (row < a_count) & (col < b_count)
        block = jnp.where(live, acc[:, j * width:(j + 1) * width], 0.0).astype(out_ref.dtype)
        out_ref[:, j] = block.reshape(parts, rows, width)


def contract(labels, amps, inter, n_irrep, j_count):
    devices, _, slab, width = amps[0].shape
    parts = devices // n_irrep
    n_k = sum(x.shape[1] for x in amps)

    def block_of(k, at):
        def index(p, labels):
            return (labels[k] ^ labels[n_k] ^ p, at, 0, 0)
        return index

    amp_ops, amp_specs, inter_specs = [], [], []
    for a in amps:
        for at in range(a.shape[1]):
            amp_specs.append(pl.BlockSpec((parts, 1, slab, width), block_of(len(amp_ops), at)))
            amp_ops.append(a)
    for k in range(n_k):
        inter_specs.append(pl.BlockSpec((parts, 1, slab, j_count * width), block_of(k, k)))
    flops = 2 * n_k * n_irrep * width ** 3 * j_count
    return pl.pallas_call(
        functools.partial(contract_kernel, n_k, width),
        grid_spec=pltpu.PrefetchScalarGridSpec(
            num_scalar_prefetch=1,
            grid=(n_irrep,),
            in_specs=amp_specs + inter_specs,
            out_specs=pl.BlockSpec((parts, j_count, slab, width), lambda p, labels: (p, 0, 0, 0)),
        ),
        out_shape=jax.ShapeDtypeStruct((devices, j_count, slab, width), jnp.bfloat16),
        compiler_params=pltpu.CompilerParams(vmem_limit_bytes=48 * 2 ** 20),
        cost_estimate=pl.CostEstimate(flops=flops, bytes_accessed=flops // 128, transcendentals=0),
    )(labels, *amp_ops, *([inter] * n_k))


def shards_any(n_batch, n_grp, amps, cycle_inter, k_irrep, i_irrep, j_irrep, virt_count):
    k_local, i_total, slab, width = amps.shape
    n_irrep = virt_count.shape[0]
    j_total = cycle_inter.shape[2]
    j_count = j_total // n_batch
    me_b = lax.axis_index("batch")
    me_g = lax.axis_index("grp")
    i_count = i_total // n_grp

    split = cycle_inter.reshape(k_local, slab, n_batch, j_count * width)
    if n_batch == 2:
        swap = [(0, 1), (1, 0)]
        own = lax.dynamic_index_in_dim(split, me_b, 2, keepdims=False)
        away = lax.dynamic_index_in_dim(split, 1 - me_b, 2, keepdims=False)
        mine = jnp.concatenate([own, lax.ppermute(away, "batch", swap)])
        k_labels = jnp.concatenate([
            lax.dynamic_slice_in_dim(k_irrep, me_b * k_local, k_local),
            lax.dynamic_slice_in_dim(k_irrep, (1 - me_b) * k_local, k_local),
        ])
    else:
        mine = lax.all_to_all(split.transpose(2, 0, 1, 3), "batch", split_axis=0, concat_axis=0, tiled=True)
        mine = mine.reshape(n_batch * k_local, slab, j_count * width)
        k_labels = k_irrep
    inter_all = lax.all_gather(mine, "grp", axis=0, tiled=False)

    sends = amps.transpose(1, 0, 2, 3).reshape(n_grp, i_count, k_local, slab, width)
    got = lax.all_to_all(sends, "grp", split_axis=0, concat_axis=0, tiled=True)
    if n_batch == 2:
        amp_parts = [got, lax.ppermute(got, "batch", swap)]
    else:
        gathered = lax.all_gather(got, "batch", axis=0, tiled=False)
        amp_parts = [gathered[b] for b in range(n_batch)]

    j_labels = lax.dynamic_slice_in_dim(j_irrep, me_b * j_count, j_count)
    outs = []
    for i in range(i_count):
        i_label = lax.dynamic_slice_in_dim(i_irrep, me_g * i_count + i, 1)
        labels = jnp.concatenate([k_labels, i_label, j_labels, virt_count])
        outs.append(contract(labels, [a[:, i] for a in amp_parts], inter_all, n_irrep, j_count))
    partial = outs[0][:, None] if i_count == 1 else jnp.stack(outs, axis=1)
    result = lax.all_to_all(partial, "grp", split_axis=0, concat_axis=0, tiled=True)
    return result.reshape(i_total, j_count, slab, width)


def tile_kernel(n_place, k_half, width, j_count, k_irrep, i_irrep, j_irrep, virt_count, *refs):
    own_refs, twin_refs = refs[:n_place], refs[n_place:2 * n_place]
    near_refs = refs[2 * n_place:3 * n_place]
    far_first, far_rest = refs[3 * n_place:3 * n_place + 2]
    far_refs = [far_first] + [far_rest.at[at] for at in range(n_place - 1)]
    out_ref, own, twin, near, far, total, sems = refs[3 * n_place + 2:]
    n_irrep = total.shape[1]
    me_b, me_g = lax.axis_index("batch"), lax.axis_index("grp")
    core, first_c = me_g % 2, me_g // 2
    i_labels = [i_irrep[2 * (me_g % (2 * n_place)) + i] for i in range(2)]
    k_labels = [k_irrep[(me_b ^ half) * k_half + k] for half in range(2) for k in range(k_half)]
    copies = []
    for at in range(n_place):
        here = []
        for which, (src, dst) in enumerate(((own_refs, own), (twin_refs, twin), (near_refs, near), (far_refs, far))):
            here.append(pltpu.make_async_copy(src[at], dst.at[at], sems.at[which, at]))
        copies.append(here)
    for here in copies:
        for copy in here:
            copy.start()
    total[...] = jnp.zeros_like(total)
    row = lax.broadcasted_iota(jnp.int32, (width, width), 0)
    col = lax.broadcasted_iota(jnp.int32, (width, width), 1)
    slot = (row + core * (width // 2)) & (width - 1)
    for at in range(n_place):
        for copy in copies[at]:
            copy.wait()
        c = first_c ^ at
        live = slot < virt_count[c]
        for half, side in enumerate((near, far)):
            for k in range(k_half):
                amps = []
                for i in range(2):
                    amp = side[at, :, k, i].reshape(width, width)
                    amps.append(jnp.where(live, amp, jnp.zeros((), amp.dtype)))
                inter = jnp.concatenate([own[at, half * k_half + k], twin[at, half * k_half + k]], axis=0)
                term = lax.dot_general(
                    jnp.concatenate(amps, axis=1), inter,
                    (((0,), (0,)), ((), ())), preferred_element_type=jnp.float32,
                )
                for i in range(2):
                    p = c ^ k_labels[half * k_half + k] ^ i_labels[i]
                    total[i, p] += term[i * width:(i + 1) * width]

    @pl.loop(0, n_irrep)
    def _(p):
        a_live = row < virt_count[p]
        for i in range(2):
            for j in range(j_count):
                b = p ^ i_labels[i] ^ j_irrep[me_b * j_count + j]
                live = a_live & (col < virt_count[b])
                block = jnp.where(live, total[i, p, :, j * width:(j + 1) * width], 0.0).astype(out_ref.dtype)
                for side in range(2):
                    out_ref[2 * p + side, i, j] = block[side * width // 2:(side + 1) * width // 2]


def shards_tiled(amps, cycle_inter, k_irrep, i_irrep, j_irrep, virt_count):
    k_half, i_total, slab, width = amps.shape
    n_irrep = virt_count.shape[0]
    j_count = cycle_inter.shape[2] // 2
    n_place = n_irrep // 2
    n_grp = 4 * n_place
    me_b = lax.axis_index("batch")
    me_g = lax.axis_index("grp")
    core, place = me_g % 2, (me_g // 2) % n_place
    swap = [(0, 1), (1, 0)]

    def flip(x, bits):
        return lax.ppermute(x, "grp", [(d, d ^ bits) for d in range(n_grp)])

    def hold(*xs):
        return lax.optimization_barrier(xs)

    def over(x):
        return lax.ppermute(x, "batch", swap)

    low, high = cycle_inter[:, :, :j_count], cycle_inter[:, :, j_count:]
    mine = jnp.where(me_b == 0, low, high).reshape(k_half, slab, j_count * width)
    away = jnp.where(me_b == 0, high, low).reshape(k_half, slab, j_count * width)
    parts = amps.reshape(k_half, n_place, 2, 2, slab, width)
    keep = lax.dynamic_index_in_dim(parts, core, 2, keepdims=False)
    take = flip(lax.dynamic_index_in_dim(parts, 1 - core, 2, keepdims=False), 1)
    i_parts = jnp.stack([keep, take])

    def i_part(at):
        return lax.dynamic_index_in_dim(i_parts, at, 2, keepdims=False)

    i_parts, away, mine = hold(i_parts, away, mine)
    other = over(away)
    near0, near1, near2, near3 = i_part(place), *(flip(i_part(place ^ m), 2 * m) for m in range(1, n_place))
    far0 = over(near0)
    own0 = jnp.concatenate([mine, other])
    own1, own2, twin0 = flip(own0, 2), flip(own0, 4), flip(own0, 1)
    far123 = over(jnp.stack([near1, near2, near3]))
    own1, own2, twin0, far0 = hold(own1, own2, twin0, far0)
    own3 = flip(own1[:k_half], 4), flip(own2[k_half:], 2)
    twin1, twin2 = flip(own1, 1), flip(own2, 1)
    far123, twin1, twin2, *own3 = hold(far123, twin1, twin2, *own3)
    own3 = jnp.concatenate(own3)
    near, far = [near0, near1, near2, near3], [far0, far123]
    own, twin = [own0, own1, own2, own3], [twin0, twin1, twin2, flip(own3, 1)]

    any_spec = pl.BlockSpec(memory_space=pl.ANY)
    flops = 2 * 2 * k_half * 2 * n_place * width ** 3 * j_count
    tile = pl.pallas_call(
        functools.partial(tile_kernel, n_place, k_half, width, j_count),
        in_specs=[pl.BlockSpec(memory_space=pltpu.SMEM)] * 4 + [any_spec] * (3 * n_place + 2),
        out_specs=pl.BlockSpec(memory_space=pltpu.VMEM),
        out_shape=jax.ShapeDtypeStruct((n_grp, 2, j_count, slab, width), jnp.bfloat16),
        scratch_shapes=[
            pltpu.VMEM((n_place, 2 * k_half, slab, j_count * width), jnp.bfloat16),
            pltpu.VMEM((n_place, 2 * k_half, slab, j_count * width), jnp.bfloat16),
            pltpu.VMEM((n_place, 2, k_half, 2, slab, width), jnp.bfloat16),
            pltpu.VMEM((n_place, 2, k_half, 2, slab, width), jnp.bfloat16),
            pltpu.VMEM((2, n_irrep, width, j_count * width), jnp.float32),
            pltpu.SemaphoreType.DMA((4, n_place)),
        ],
        compiler_params=pltpu.CompilerParams(vmem_limit_bytes=24 * 2 ** 20),
        cost_estimate=pl.CostEstimate(flops=flops, bytes_accessed=8 * 2 ** 20, transcendentals=0),
    )(k_irrep, i_irrep, j_irrep, virt_count, *own, *twin, *near, *far)
    result = lax.all_to_all(tile, "grp", split_axis=0, concat_axis=0, tiled=True)
    result = result.reshape(2, i_total, j_count, slab, width).astype(jnp.float32)
    return (result[0] + result[1]).astype(jnp.bfloat16)


def shards(n_batch, n_grp, amps, cycle_inter, k_irrep, i_irrep, j_irrep, virt_count):
    operands = (amps, cycle_inter, k_irrep, i_irrep, j_irrep, virt_count)
    n_irrep = virt_count.shape[0]
    if n_batch == 2 and n_grp == 2 * n_irrep and n_irrep == 8 and amps.shape[1] == n_grp:
        return shards_tiled(*operands)
    return shards_any(n_batch, n_grp, *operands)


def solution(mesh):
    return jax.shard_map(
        functools.partial(shards, mesh.shape["batch"], mesh.shape["grp"]),
        mesh=mesh,
        in_specs=(P("batch", None, "grp", None), P("batch", "grp", None, None), P(), P(), P(), P()),
        out_specs=P(None, "batch", "grp", None),
        check_vma=False,
    )
```

```python
import functools

import jax
import jax.numpy as jnp
from jax import lax
from jax.experimental import pallas as pl
from jax.experimental.pallas import tpu as pltpu
from jax.sharding import PartitionSpec as P


def contract_kernel(n_k, width, labels_ref, *refs):
    amp_refs = refs[:n_k]
    inter_refs = refs[n_k:2 * n_k]
    out_ref = refs[2 * n_k]
    p = pl.program_id(0)
    n_irrep = pl.num_programs(0)
    j_count = out_ref.shape[1]
    i_label = labels_ref[n_k]
    j_first = n_k + 1
    count_first = j_first + j_count
    row = lax.broadcasted_iota(jnp.int32, (width, width), 0)
    col = lax.broadcasted_iota(jnp.int32, (width, width), 1)
    acc = None
    for k in range(n_k):
        c_count = labels_ref[count_first + (labels_ref[k] ^ i_label ^ p)]
        amp = amp_refs[k][...].reshape(width, width)
        amp = jnp.where(row < c_count, amp, jnp.zeros((), amp.dtype))
        inter = inter_refs[k][...].reshape(width, j_count * width)
        term = lax.dot_general(amp, inter, (((0,), (0,)), ((), ())), preferred_element_type=jnp.float32)
        acc = term if acc is None else acc + term
    a_count = labels_ref[count_first + p]
    parts, rows = out_ref.shape[0], out_ref.shape[2]
    for j in range(j_count):
        b_count = labels_ref[count_first + (p ^ i_label ^ labels_ref[j_first + j])]
        live = (row < a_count) & (col < b_count)
        block = jnp.where(live, acc[:, j * width:(j + 1) * width], 0.0).astype(out_ref.dtype)
        out_ref[:, j] = block.reshape(parts, rows, width)


def contract(labels, amps, inter, n_irrep, j_count):
    devices, _, slab, width = amps[0].shape
    parts = devices // n_irrep
    n_k = sum(x.shape[1] for x in amps)

    def block_of(k, at):
        def index(p, labels):
            return (labels[k] ^ labels[n_k] ^ p, at, 0, 0)
        return index

    amp_ops, amp_specs, inter_specs = [], [], []
    for a in amps:
        for at in range(a.shape[1]):
            amp_specs.append(pl.BlockSpec((parts, 1, slab, width), block_of(len(amp_ops), at)))
            amp_ops.append(a)
    for k in range(n_k):
        inter_specs.append(pl.BlockSpec((parts, 1, slab, j_count * width), block_of(k, k)))
    flops = 2 * n_k * n_irrep * width ** 3 * j_count
    return pl.pallas_call(
        functools.partial(contract_kernel, n_k, width),
        grid_spec=pltpu.PrefetchScalarGridSpec(
            num_scalar_prefetch=1,
            grid=(n_irrep,),
            in_specs=amp_specs + inter_specs,
            out_specs=pl.BlockSpec((parts, j_count, slab, width), lambda p, labels: (p, 0, 0, 0)),
        ),
        out_shape=jax.ShapeDtypeStruct((devices, j_count, slab, width), jnp.bfloat16),
        compiler_params=pltpu.CompilerParams(vmem_limit_bytes=48 * 2 ** 20),
        cost_estimate=pl.CostEstimate(flops=flops, bytes_accessed=flops // 128, transcendentals=0),
    )(labels, *amp_ops, *([inter] * n_k))


def shards_any(n_batch, n_grp, amps, cycle_inter, k_irrep, i_irrep, j_irrep, virt_count):
    k_local, i_total, slab, width = amps.shape
    n_irrep = virt_count.shape[0]
    j_total = cycle_inter.shape[2]
    j_count = j_total // n_batch
    me_b = lax.axis_index("batch")
    me_g = lax.axis_index("grp")
    i_count = i_total // n_grp

    split = cycle_inter.reshape(k_local, slab, n_batch, j_count * width)
    if n_batch == 2:
        swap = [(0, 1), (1, 0)]
        own = lax.dynamic_index_in_dim(split, me_b, 2, keepdims=False)
        away = lax.dynamic_index_in_dim(split, 1 - me_b, 2, keepdims=False)
        mine = jnp.concatenate([own, lax.ppermute(away, "batch", swap)])
        k_labels = jnp.concatenate([
            lax.dynamic_slice_in_dim(k_irrep, me_b * k_local, k_local),
            lax.dynamic_slice_in_dim(k_irrep, (1 - me_b) * k_local, k_local),
        ])
    else:
        mine = lax.all_to_all(split.transpose(2, 0, 1, 3), "batch", split_axis=0, concat_axis=0, tiled=True)
        mine = mine.reshape(n_batch * k_local, slab, j_count * width)
        k_labels = k_irrep
    inter_all = lax.all_gather(mine, "grp", axis=0, tiled=False)

    sends = amps.transpose(1, 0, 2, 3).reshape(n_grp, i_count, k_local, slab, width)
    got = lax.all_to_all(sends, "grp", split_axis=0, concat_axis=0, tiled=True)
    if n_batch == 2:
        amp_parts = [got, lax.ppermute(got, "batch", swap)]
    else:
        gathered = lax.all_gather(got, "batch", axis=0, tiled=False)
        amp_parts = [gathered[b] for b in range(n_batch)]

    j_labels = lax.dynamic_slice_in_dim(j_irrep, me_b * j_count, j_count)
    outs = []
    for i in range(i_count):
        i_label = lax.dynamic_slice_in_dim(i_irrep, me_g * i_count + i, 1)
        labels = jnp.concatenate([k_labels, i_label, j_labels, virt_count])
        outs.append(contract(labels, [a[:, i] for a in amp_parts], inter_all, n_irrep, j_count))
    partial = outs[0][:, None] if i_count == 1 else jnp.stack(outs, axis=1)
    result = lax.all_to_all(partial, "grp", split_axis=0, concat_axis=0, tiled=True)
    return result.reshape(i_total, j_count, slab, width)


def tile_kernel(n_place, k_half, width, j_count, k_irrep, i_irrep, j_irrep, virt_count, *refs):
    own, twin, near = refs[:n_place], refs[n_place:2 * n_place], refs[2 * n_place:3 * n_place]
    far_first, far_rest, out_ref, total = refs[3 * n_place:]
    far = [far_first] + [far_rest.at[at] for at in range(n_place - 1)]
    n_irrep = total.shape[1]
    me_b, me_g = lax.axis_index("batch"), lax.axis_index("grp")
    core, first_c = me_g % 2, me_g // 2
    i_labels = [i_irrep[2 * (me_g % (2 * n_place)) + i] for i in range(2)]
    k_labels = [k_irrep[(me_b ^ half) * k_half + k] for half in range(2) for k in range(k_half)]
    total[...] = jnp.zeros_like(total)
    row = lax.broadcasted_iota(jnp.int32, (width, width), 0)
    col = lax.broadcasted_iota(jnp.int32, (width, width), 1)
    slot = (row + core * (width // 2)) & (width - 1)
    for at in range(n_place):
        c = first_c ^ at
        live = slot < virt_count[c]
        for half, side in enumerate((near, far)):
            for k in range(k_half):
                amps = []
                for i in range(2):
                    amp = side[at][:, k, i].reshape(width, width)
                    amps.append(jnp.where(live, amp, jnp.zeros((), amp.dtype)))
                inter = jnp.concatenate([own[at][half * k_half + k], twin[at][half * k_half + k]], axis=0)
                term = lax.dot_general(
                    jnp.concatenate(amps, axis=1), inter,
                    (((0,), (0,)), ((), ())), preferred_element_type=jnp.float32,
                )
                for i in range(2):
                    p = c ^ k_labels[half * k_half + k] ^ i_labels[i]
                    total[i, p] += term[i * width:(i + 1) * width]

    @pl.loop(0, n_irrep)
    def _(p):
        a_live = row < virt_count[p]
        for i in range(2):
            for j in range(j_count):
                b = p ^ i_labels[i] ^ j_irrep[me_b * j_count + j]
                live = a_live & (col < virt_count[b])
                block = jnp.where(live, total[i, p, :, j * width:(j + 1) * width], 0.0).astype(out_ref.dtype)
                for side in range(2):
                    out_ref[2 * p + side, i, j] = block[side * width // 2:(side + 1) * width // 2]


def shards_tiled(amps, cycle_inter, k_irrep, i_irrep, j_irrep, virt_count):
    k_half, i_total, slab, width = amps.shape
    n_irrep = virt_count.shape[0]
    j_count = cycle_inter.shape[2] // 2
    n_place = n_irrep // 2
    n_grp = 4 * n_place
    me_b = lax.axis_index("batch")
    me_g = lax.axis_index("grp")
    core, place = me_g % 2, (me_g // 2) % n_place
    swap = [(0, 1), (1, 0)]

    def flip(x, bits):
        return lax.ppermute(x, "grp", [(d, d ^ bits) for d in range(n_grp)])

    def hold(*xs):
        return lax.optimization_barrier(xs)

    def over(x):
        return lax.ppermute(x, "batch", swap)

    low, high = cycle_inter[:, :, :j_count], cycle_inter[:, :, j_count:]
    mine = jnp.where(me_b == 0, low, high).reshape(k_half, slab, j_count * width)
    away = jnp.where(me_b == 0, high, low).reshape(k_half, slab, j_count * width)
    parts = amps.reshape(k_half, n_place, 2, 2, slab, width)
    keep = lax.dynamic_index_in_dim(parts, core, 2, keepdims=False)
    take = flip(lax.dynamic_index_in_dim(parts, 1 - core, 2, keepdims=False), 1)
    i_parts = jnp.stack([keep, take])

    def i_part(at):
        return lax.dynamic_index_in_dim(i_parts, at, 2, keepdims=False)

    i_parts, away, mine = hold(i_parts, away, mine)
    other = over(away)
    near0, near1, near2, near3 = i_part(place), *(flip(i_part(place ^ m), 2 * m) for m in range(1, n_place))
    far0 = over(near0)
    own0 = jnp.concatenate([mine, other])
    own1, own2, twin0 = flip(own0, 2), flip(own0, 4), flip(own0, 1)
    far123 = over(jnp.stack([near1, near2, near3]))
    own1, own2, twin0, far0 = hold(own1, own2, twin0, far0)
    own3 = flip(own1[:k_half], 4), flip(own2[k_half:], 2)
    twin1, twin2 = flip(own1, 1), flip(own2, 1)
    far123, twin1, twin2, *own3 = hold(far123, twin1, twin2, *own3)
    own3 = jnp.concatenate(own3)
    near, far = [near0, near1, near2, near3], [far0, far123]
    own, twin = [own0, own1, own2, own3], [twin0, twin1, twin2, flip(own3, 1)]

    here = pl.BlockSpec(memory_space=pltpu.VMEM)
    flops = 2 * 2 * k_half * 2 * n_place * width ** 3 * j_count
    tile = pl.pallas_call(
        functools.partial(tile_kernel, n_place, k_half, width, j_count),
        in_specs=[pl.BlockSpec(memory_space=pltpu.SMEM)] * 4 + [here] * (3 * n_place + 2),
        out_specs=here,
        out_shape=jax.ShapeDtypeStruct((n_grp, 2, j_count, slab, width), jnp.bfloat16),
        scratch_shapes=[pltpu.VMEM((2, n_irrep, width, j_count * width), jnp.float32)],
        compiler_params=pltpu.CompilerParams(vmem_limit_bytes=16 * 2 ** 20),
        cost_estimate=pl.CostEstimate(flops=flops, bytes_accessed=8 * 2 ** 20, transcendentals=0),
    )(k_irrep, i_irrep, j_irrep, virt_count, *own, *twin, *near, *far)
    result = lax.all_to_all(tile, "grp", split_axis=0, concat_axis=0, tiled=True)
    result = result.reshape(2, i_total, j_count, slab, width).astype(jnp.float32)
    return (result[0] + result[1]).astype(jnp.bfloat16)


def shards(n_batch, n_grp, amps, cycle_inter, k_irrep, i_irrep, j_irrep, virt_count):
    operands = (amps, cycle_inter, k_irrep, i_irrep, j_irrep, virt_count)
    n_irrep = virt_count.shape[0]
    if n_batch == 2 and n_grp == 2 * n_irrep and n_irrep == 8 and amps.shape[1] == n_grp:
        return shards_tiled(*operands)
    return shards_any(n_batch, n_grp, *operands)


def solution(mesh):
    return jax.shard_map(
        functools.partial(shards, mesh.shape["batch"], mesh.shape["grp"]),
        mesh=mesh,
        in_specs=(P("batch", None, "grp", None), P("batch", "grp", None, None), P(), P(), P(), P()),
        out_specs=P(None, "batch", "grp", None),
        check_vma=False,
    )
```

```python
import functools

import jax
import jax.numpy as jnp
from jax import lax
from jax.experimental import pallas as pl
from jax.experimental.pallas import tpu as pltpu
from jax.sharding import PartitionSpec as P


def contract_kernel(n_k, width, labels_ref, *refs):
    amp_refs = refs[:n_k]
    inter_refs = refs[n_k:2 * n_k]
    out_ref = refs[2 * n_k]
    p = pl.program_id(0)
    n_irrep = pl.num_programs(0)
    j_count = out_ref.shape[1]
    i_label = labels_ref[n_k]
    j_first = n_k + 1
    count_first = j_first + j_count
    row = lax.broadcasted_iota(jnp.int32, (width, width), 0)
    col = lax.broadcasted_iota(jnp.int32, (width, width), 1)
    acc = None
    for k in range(n_k):
        c_count = labels_ref[count_first + (labels_ref[k] ^ i_label ^ p)]
        amp = amp_refs[k][...].reshape(width, width)
        amp = jnp.where(row < c_count, amp, jnp.zeros((), amp.dtype))
        inter = inter_refs[k][...].reshape(width, j_count * width)
        term = lax.dot_general(amp, inter, (((0,), (0,)), ((), ())), preferred_element_type=jnp.float32)
        acc = term if acc is None else acc + term
    a_count = labels_ref[count_first + p]
    parts, rows = out_ref.shape[0], out_ref.shape[2]
    for j in range(j_count):
        b_count = labels_ref[count_first + (p ^ i_label ^ labels_ref[j_first + j])]
        live = (row < a_count) & (col < b_count)
        block = jnp.where(live, acc[:, j * width:(j + 1) * width], 0.0).astype(out_ref.dtype)
        out_ref[:, j] = block.reshape(parts, rows, width)


def contract(labels, amps, inter, n_irrep, j_count):
    devices, _, slab, width = amps[0].shape
    parts = devices // n_irrep
    n_k = sum(x.shape[1] for x in amps)

    def block_of(k, at):
        def index(p, labels):
            return (labels[k] ^ labels[n_k] ^ p, at, 0, 0)
        return index

    amp_ops, amp_specs, inter_specs = [], [], []
    for a in amps:
        for at in range(a.shape[1]):
            amp_specs.append(pl.BlockSpec((parts, 1, slab, width), block_of(len(amp_ops), at)))
            amp_ops.append(a)
    for k in range(n_k):
        inter_specs.append(pl.BlockSpec((parts, 1, slab, j_count * width), block_of(k, k)))
    flops = 2 * n_k * n_irrep * width ** 3 * j_count
    return pl.pallas_call(
        functools.partial(contract_kernel, n_k, width),
        grid_spec=pltpu.PrefetchScalarGridSpec(
            num_scalar_prefetch=1,
            grid=(n_irrep,),
            in_specs=amp_specs + inter_specs,
            out_specs=pl.BlockSpec((parts, j_count, slab, width), lambda p, labels: (p, 0, 0, 0)),
        ),
        out_shape=jax.ShapeDtypeStruct((devices, j_count, slab, width), jnp.bfloat16),
        compiler_params=pltpu.CompilerParams(vmem_limit_bytes=48 * 2 ** 20),
        cost_estimate=pl.CostEstimate(flops=flops, bytes_accessed=flops // 128, transcendentals=0),
    )(labels, *amp_ops, *([inter] * n_k))


def shards_any(n_batch, n_grp, amps, cycle_inter, k_irrep, i_irrep, j_irrep, virt_count):
    k_local, i_total, slab, width = amps.shape
    n_irrep = virt_count.shape[0]
    j_total = cycle_inter.shape[2]
    j_count = j_total // n_batch
    me_b = lax.axis_index("batch")
    me_g = lax.axis_index("grp")
    i_count = i_total // n_grp

    split = cycle_inter.reshape(k_local, slab, n_batch, j_count * width)
    if n_batch == 2:
        swap = [(0, 1), (1, 0)]
        own = lax.dynamic_index_in_dim(split, me_b, 2, keepdims=False)
        away = lax.dynamic_index_in_dim(split, 1 - me_b, 2, keepdims=False)
        mine = jnp.concatenate([own, lax.ppermute(away, "batch", swap)])
        k_labels = jnp.concatenate([
            lax.dynamic_slice_in_dim(k_irrep, me_b * k_local, k_local),
            lax.dynamic_slice_in_dim(k_irrep, (1 - me_b) * k_local, k_local),
        ])
    else:
        mine = lax.all_to_all(split.transpose(2, 0, 1, 3), "batch", split_axis=0, concat_axis=0, tiled=True)
        mine = mine.reshape(n_batch * k_local, slab, j_count * width)
        k_labels = k_irrep
    inter_all = lax.all_gather(mine, "grp", axis=0, tiled=False)

    sends = amps.transpose(1, 0, 2, 3).reshape(n_grp, i_count, k_local, slab, width)
    got = lax.all_to_all(sends, "grp", split_axis=0, concat_axis=0, tiled=True)
    if n_batch == 2:
        amp_parts = [got, lax.ppermute(got, "batch", swap)]
    else:
        gathered = lax.all_gather(got, "batch", axis=0, tiled=False)
        amp_parts = [gathered[b] for b in range(n_batch)]

    j_labels = lax.dynamic_slice_in_dim(j_irrep, me_b * j_count, j_count)
    outs = []
    for i in range(i_count):
        i_label = lax.dynamic_slice_in_dim(i_irrep, me_g * i_count + i, 1)
        labels = jnp.concatenate([k_labels, i_label, j_labels, virt_count])
        outs.append(contract(labels, [a[:, i] for a in amp_parts], inter_all, n_irrep, j_count))
    partial = outs[0][:, None] if i_count == 1 else jnp.stack(outs, axis=1)
    result = lax.all_to_all(partial, "grp", split_axis=0, concat_axis=0, tiled=True)
    return result.reshape(i_total, j_count, slab, width)


def tile_kernel(n_place, k_half, width, j_count, k_irrep, i_irrep, j_irrep, virt_count, *refs):
    own, twin, near = refs[:n_place], refs[n_place:2 * n_place], refs[2 * n_place:3 * n_place]
    far_first, far_rest, out_ref, total = refs[3 * n_place:]
    far = [far_first] + [far_rest.at[at] for at in range(n_place - 1)]
    n_irrep = total.shape[1]
    me_b, me_g = lax.axis_index("batch"), lax.axis_index("grp")
    core, first_c = me_g % 2, me_g // 2
    i_labels = [i_irrep[2 * (me_g % (2 * n_place)) + i] for i in range(2)]
    k_labels = [k_irrep[(me_b ^ half) * k_half + k] for half in range(2) for k in range(k_half)]
    total[...] = jnp.zeros_like(total)
    row = lax.broadcasted_iota(jnp.int32, (width, width), 0)
    col = lax.broadcasted_iota(jnp.int32, (width, width), 1)
    slot = (row + core * (width // 2)) & (width - 1)
    for at in range(n_place):
        c = first_c ^ at
        live = slot < virt_count[c]
        for half, side in enumerate((near, far)):
            for k in range(k_half):
                amps = []
                for i in range(2):
                    amp = side[at][:, k, i].reshape(width, width)
                    amps.append(jnp.where(live, amp, jnp.zeros((), amp.dtype)))
                inter = jnp.concatenate([own[at][half * k_half + k], twin[at][half * k_half + k]], axis=0)
                term = lax.dot_general(
                    jnp.concatenate(amps, axis=1), inter,
                    (((0,), (0,)), ((), ())), preferred_element_type=jnp.float32,
                )
                for i in range(2):
                    p = c ^ k_labels[half * k_half + k] ^ i_labels[i]
                    total[i, p] += term[i * width:(i + 1) * width]

    @pl.loop(0, n_irrep)
    def _(p):
        a_live = row < virt_count[p]
        for i in range(2):
            for j in range(j_count):
                b = p ^ i_labels[i] ^ j_irrep[me_b * j_count + j]
                live = a_live & (col < virt_count[b])
                block = jnp.where(live, total[i, p, :, j * width:(j + 1) * width], 0.0).astype(out_ref.dtype)
                for side in range(2):
                    out_ref[2 * p + side, i, j] = block[side * width // 2:(side + 1) * width // 2]


def shards_tiled(amps, cycle_inter, k_irrep, i_irrep, j_irrep, virt_count):
    k_half, i_total, slab, width = amps.shape
    n_irrep = virt_count.shape[0]
    j_count = cycle_inter.shape[2] // 2
    n_place = n_irrep // 2
    n_grp = 4 * n_place
    me_b = lax.axis_index("batch")
    me_g = lax.axis_index("grp")
    core, place = me_g % 2, (me_g // 2) % n_place
    swap = [(0, 1), (1, 0)]

    def flip(x, bits):
        return lax.ppermute(x, "grp", [(d, d ^ bits) for d in range(n_grp)])

    def hold(*xs):
        return lax.optimization_barrier(xs)

    def over(x):
        return lax.ppermute(x, "batch", swap)

    low, high = cycle_inter[:, :, :j_count], cycle_inter[:, :, j_count:]
    mine = jnp.where(me_b == 0, low, high).reshape(k_half, slab, j_count * width)
    away = jnp.where(me_b == 0, high, low).reshape(k_half, slab, j_count * width)
    parts = amps.reshape(k_half, n_place, 2, 2, slab, width)
    keep = lax.dynamic_index_in_dim(parts, core, 2, keepdims=False)
    take = flip(lax.dynamic_index_in_dim(parts, 1 - core, 2, keepdims=False), 1)
    i_parts = jnp.stack([keep, take])

    def i_part(at):
        return lax.dynamic_index_in_dim(i_parts, at, 2, keepdims=False)

    other = over(away)
    near0, near1, near2, near3 = i_part(place), *(flip(i_part(place ^ m), 2 * m) for m in range(1, n_place))
    far0 = over(near0)
    other, near1 = hold(other, near1)
    near1, near2, near3, far0 = hold(near1, near2, near3, far0)
    own0 = jnp.concatenate([mine, other])
    own1, own2, twin0 = flip(own0, 2), flip(own0, 4), flip(own0, 1)
    far123 = over(jnp.stack([near1, near2, near3]))
    own1, own2, twin0 = hold(own1, own2, twin0)
    own3 = flip(own1[:k_half], 4), flip(own2[k_half:], 2)
    twin1, twin2 = flip(own1, 1), flip(own2, 1)
    far123, twin1, twin2, *own3 = hold(far123, twin1, twin2, *own3)
    own3 = jnp.concatenate(own3)
    near, far = [near0, near1, near2, near3], [far0, far123]
    own, twin = [own0, own1, own2, own3], [twin0, twin1, twin2, flip(own3, 1)]

    here = pl.BlockSpec(memory_space=pltpu.VMEM)
    flops = 2 * 2 * k_half * 2 * n_place * width ** 3 * j_count
    tile = pl.pallas_call(
        functools.partial(tile_kernel, n_place, k_half, width, j_count),
        in_specs=[pl.BlockSpec(memory_space=pltpu.SMEM)] * 4 + [here] * (3 * n_place + 2),
        out_specs=here,
        out_shape=jax.ShapeDtypeStruct((n_grp, 2, j_count, slab, width), jnp.bfloat16),
        scratch_shapes=[pltpu.VMEM((2, n_irrep, width, j_count * width), jnp.float32)],
        compiler_params=pltpu.CompilerParams(vmem_limit_bytes=16 * 2 ** 20),
        cost_estimate=pl.CostEstimate(flops=flops, bytes_accessed=8 * 2 ** 20, transcendentals=0),
    )(k_irrep, i_irrep, j_irrep, virt_count, *own, *twin, *near, *far)
    result = lax.all_to_all(tile, "grp", split_axis=0, concat_axis=0, tiled=True)
    result = result.reshape(2, i_total, j_count, slab, width)
    return result[0] + result[1]


def shards(n_batch, n_grp, amps, cycle_inter, k_irrep, i_irrep, j_irrep, virt_count):
    operands = (amps, cycle_inter, k_irrep, i_irrep, j_irrep, virt_count)
    n_irrep = virt_count.shape[0]
    if n_batch == 2 and n_grp == 2 * n_irrep and n_irrep == 8 and amps.shape[1] == n_grp:
        return shards_tiled(*operands)
    return shards_any(n_batch, n_grp, *operands)


def solution(mesh):
    return jax.shard_map(
        functools.partial(shards, mesh.shape["batch"], mesh.shape["grp"]),
        mesh=mesh,
        in_specs=(P("batch", None, "grp", None), P("batch", "grp", None, None), P(), P(), P(), P()),
        out_specs=P(None, "batch", "grp", None),
        check_vma=False,
    )
```

```python
import functools

import jax
import jax.numpy as jnp
from jax import lax
from jax.experimental import pallas as pl
from jax.experimental.pallas import tpu as pltpu
from jax.sharding import PartitionSpec as P


def contract_kernel(n_k, width, labels_ref, *refs):
    amp_refs = refs[:n_k]
    inter_refs = refs[n_k:2 * n_k]
    out_ref = refs[2 * n_k]
    p = pl.program_id(0)
    n_irrep = pl.num_programs(0)
    j_count = out_ref.shape[1]
    i_label = labels_ref[n_k]
    j_first = n_k + 1
    count_first = j_first + j_count
    row = lax.broadcasted_iota(jnp.int32, (width, width), 0)
    col = lax.broadcasted_iota(jnp.int32, (width, width), 1)
    acc = None
    for k in range(n_k):
        c_count = labels_ref[count_first + (labels_ref[k] ^ i_label ^ p)]
        amp = amp_refs[k][...].reshape(width, width)
        amp = jnp.where(row < c_count, amp, jnp.zeros((), amp.dtype))
        inter = inter_refs[k][...].reshape(width, j_count * width)
        term = lax.dot_general(amp, inter, (((0,), (0,)), ((), ())), preferred_element_type=jnp.float32)
        acc = term if acc is None else acc + term
    a_count = labels_ref[count_first + p]
    parts, rows = out_ref.shape[0], out_ref.shape[2]
    for j in range(j_count):
        b_count = labels_ref[count_first + (p ^ i_label ^ labels_ref[j_first + j])]
        live = (row < a_count) & (col < b_count)
        block = jnp.where(live, acc[:, j * width:(j + 1) * width], 0.0).astype(out_ref.dtype)
        out_ref[:, j] = block.reshape(parts, rows, width)


def contract(labels, amps, inter, n_irrep, j_count):
    devices, _, slab, width = amps[0].shape
    parts = devices // n_irrep
    n_k = sum(x.shape[1] for x in amps)

    def block_of(k, at):
        def index(p, labels):
            return (labels[k] ^ labels[n_k] ^ p, at, 0, 0)
        return index

    amp_ops, amp_specs, inter_specs = [], [], []
    for a in amps:
        for at in range(a.shape[1]):
            amp_specs.append(pl.BlockSpec((parts, 1, slab, width), block_of(len(amp_ops), at)))
            amp_ops.append(a)
    for k in range(n_k):
        inter_specs.append(pl.BlockSpec((parts, 1, slab, j_count * width), block_of(k, k)))
    flops = 2 * n_k * n_irrep * width ** 3 * j_count
    return pl.pallas_call(
        functools.partial(contract_kernel, n_k, width),
        grid_spec=pltpu.PrefetchScalarGridSpec(
            num_scalar_prefetch=1,
            grid=(n_irrep,),
            in_specs=amp_specs + inter_specs,
            out_specs=pl.BlockSpec((parts, j_count, slab, width), lambda p, labels: (p, 0, 0, 0)),
        ),
        out_shape=jax.ShapeDtypeStruct((devices, j_count, slab, width), jnp.bfloat16),
        compiler_params=pltpu.CompilerParams(vmem_limit_bytes=48 * 2 ** 20),
        cost_estimate=pl.CostEstimate(flops=flops, bytes_accessed=flops // 128, transcendentals=0),
    )(labels, *amp_ops, *([inter] * n_k))


def shards_any(n_batch, n_grp, amps, cycle_inter, k_irrep, i_irrep, j_irrep, virt_count):
    k_local, i_total, slab, width = amps.shape
    n_irrep = virt_count.shape[0]
    j_total = cycle_inter.shape[2]
    j_count = j_total // n_batch
    me_b = lax.axis_index("batch")
    me_g = lax.axis_index("grp")
    i_count = i_total // n_grp

    split = cycle_inter.reshape(k_local, slab, n_batch, j_count * width)
    if n_batch == 2:
        swap = [(0, 1), (1, 0)]
        own = lax.dynamic_index_in_dim(split, me_b, 2, keepdims=False)
        away = lax.dynamic_index_in_dim(split, 1 - me_b, 2, keepdims=False)
        mine = jnp.concatenate([own, lax.ppermute(away, "batch", swap)])
        k_labels = jnp.concatenate([
            lax.dynamic_slice_in_dim(k_irrep, me_b * k_local, k_local),
            lax.dynamic_slice_in_dim(k_irrep, (1 - me_b) * k_local, k_local),
        ])
    else:
        mine = lax.all_to_all(split.transpose(2, 0, 1, 3), "batch", split_axis=0, concat_axis=0, tiled=True)
        mine = mine.reshape(n_batch * k_local, slab, j_count * width)
        k_labels = k_irrep
    inter_all = lax.all_gather(mine, "grp", axis=0, tiled=False)

    sends = amps.transpose(1, 0, 2, 3).reshape(n_grp, i_count, k_local, slab, width)
    got = lax.all_to_all(sends, "grp", split_axis=0, concat_axis=0, tiled=True)
    if n_batch == 2:
        amp_parts = [got, lax.ppermute(got, "batch", swap)]
    else:
        gathered = lax.all_gather(got, "batch", axis=0, tiled=False)
        amp_parts = [gathered[b] for b in range(n_batch)]

    j_labels = lax.dynamic_slice_in_dim(j_irrep, me_b * j_count, j_count)
    outs = []
    for i in range(i_count):
        i_label = lax.dynamic_slice_in_dim(i_irrep, me_g * i_count + i, 1)
        labels = jnp.concatenate([k_labels, i_label, j_labels, virt_count])
        outs.append(contract(labels, [a[:, i] for a in amp_parts], inter_all, n_irrep, j_count))
    partial = outs[0][:, None] if i_count == 1 else jnp.stack(outs, axis=1)
    result = lax.all_to_all(partial, "grp", split_axis=0, concat_axis=0, tiled=True)
    return result.reshape(i_total, j_count, slab, width)


def device_labels(n_place, k_half, k_irrep, i_irrep):
    me_b, me_g = lax.axis_index("batch"), lax.axis_index("grp")
    i_labels = [i_irrep[2 * (me_g % (2 * n_place)) + i] for i in range(2)]
    k_labels = [k_irrep[(me_b ^ half) * k_half + k] for half in range(2) for k in range(k_half)]
    return me_b, me_g % 2, me_g // 2, k_labels, i_labels


def add_terms(n_place, k_half, pieces, k_irrep, i_irrep, virt_count, total):
    width = total.shape[2]
    _, core, first_c, k_labels, i_labels = device_labels(n_place, k_half, k_irrep, i_irrep)
    row = lax.broadcasted_iota(jnp.int32, (width, width), 0)
    slot = (row + core * (width // 2)) & (width - 1)
    for at, half, side, own, twin in pieces:
        c = first_c ^ at
        live = slot < virt_count[c]
        for k in range(k_half):
            amps = []
            for i in range(2):
                amp = side[:, k, i].reshape(width, width)
                amps.append(jnp.where(live, amp, jnp.zeros((), amp.dtype)))
            inter = jnp.concatenate([own[half * k_half + k], twin[half * k_half + k]], axis=0)
            term = lax.dot_general(
                jnp.concatenate(amps, axis=1), inter, (((0,), (0,)), ((), ())), preferred_element_type=jnp.float32
            )
            for i in range(2):
                p = c ^ k_labels[half * k_half + k] ^ i_labels[i]
                total[i, p] += term[i * width:(i + 1) * width]


def early_kernel(n_place, k_half, k_irrep, i_irrep, virt_count, *refs):
    m = n_place - 1
    own, twin, near, (far, total) = refs[:m], refs[m:2 * m], refs[2 * m:3 * m], refs[3 * m:]
    total[...] = jnp.zeros_like(total)
    pieces = [(at, 0, near[at], own[at], twin[at]) for at in range(m)] + [(0, 1, far, own[0], twin[0])]
    add_terms(n_place, k_half, pieces, k_irrep, i_irrep, virt_count, total)


def late_kernel(n_place, k_half, k_irrep, i_irrep, virt_count, j_irrep, *refs):
    m = n_place - 1
    own, twin, (near, far, _, out_ref, total) = refs[:m], refs[m:2 * m], refs[2 * m:]
    n_irrep, width = total.shape[1:3]
    j_count = out_ref.shape[2]
    pieces = [(at, 1, far.at[at - 1], own[at - 1], twin[at - 1]) for at in range(1, n_place)]
    pieces.append((m, 0, near, own[m - 1], twin[m - 1]))
    add_terms(n_place, k_half, pieces, k_irrep, i_irrep, virt_count, total)
    me_b, _, _, _, i_labels = device_labels(n_place, k_half, k_irrep, i_irrep)
    row = lax.broadcasted_iota(jnp.int32, (width, width), 0)
    col = lax.broadcasted_iota(jnp.int32, (width, width), 1)

    @pl.loop(0, n_irrep)
    def _(p):
        a_live = row < virt_count[p]
        for i in range(2):
            for j in range(j_count):
                b = p ^ i_labels[i] ^ j_irrep[me_b * j_count + j]
                live = a_live & (col < virt_count[b])
                block = jnp.where(live, total[i, p, :, j * width:(j + 1) * width], 0.0).astype(out_ref.dtype)
                for side in range(2):
                    out_ref[2 * p + side, i, j] = block[side * width // 2:(side + 1) * width // 2]


def shards_tiled(amps, cycle_inter, k_irrep, i_irrep, j_irrep, virt_count):
    k_half, i_total, slab, width = amps.shape
    n_irrep = virt_count.shape[0]
    j_count = cycle_inter.shape[2] // 2
    n_place = n_irrep // 2
    n_grp = 4 * n_place
    me_b = lax.axis_index("batch")
    me_g = lax.axis_index("grp")
    core, place = me_g % 2, (me_g // 2) % n_place
    swap = [(0, 1), (1, 0)]

    def flip(x, bits):
        return lax.ppermute(x, "grp", [(d, d ^ bits) for d in range(n_grp)])

    def hold(*xs):
        return lax.optimization_barrier(xs)

    def over(x):
        return lax.ppermute(x, "batch", swap)

    low, high = cycle_inter[:, :, :j_count], cycle_inter[:, :, j_count:]
    mine = jnp.where(me_b == 0, low, high).reshape(k_half, slab, j_count * width)
    away = jnp.where(me_b == 0, high, low).reshape(k_half, slab, j_count * width)
    parts = amps.reshape(k_half, n_place, 2, 2, slab, width)
    keep = lax.dynamic_index_in_dim(parts, core, 2, keepdims=False)
    take = flip(lax.dynamic_index_in_dim(parts, 1 - core, 2, keepdims=False), 1)
    i_parts = jnp.stack([keep, take])

    def i_part(at):
        return lax.dynamic_index_in_dim(i_parts, at, 2, keepdims=False)

    other = over(away)
    near0, near1, near2, near3 = i_part(place), *(flip(i_part(place ^ m), 2 * m) for m in range(1, n_place))
    far0 = over(near0)
    other, near1 = hold(other, near1)
    near1, near2, near3, far0 = hold(near1, near2, near3, far0)
    own0 = jnp.concatenate([mine, other])
    own1, own2, twin0 = flip(own0, 2), flip(own0, 4), flip(own0, 1)
    far123 = over(jnp.stack([near1, near2, near3]))
    own1, own2, twin0 = hold(own1, own2, twin0)
    own3 = flip(own1[:k_half], 4), flip(own2[k_half:], 2)
    twin1, twin2 = flip(own1, 1), flip(own2, 1)
    here, scalars = pl.BlockSpec(memory_space=pltpu.VMEM), pl.BlockSpec(memory_space=pltpu.SMEM)
    terms = jax.ShapeDtypeStruct((2, n_irrep, width, j_count * width), jnp.float32)
    flops = 2 * k_half * 2 * n_place * width ** 3 * j_count
    cost = pl.CostEstimate(flops=flops, bytes_accessed=2 ** 20, transcendentals=0)
    params = pltpu.CompilerParams(vmem_limit_bytes=16 * 2 ** 20)
    operands = [own0, own1, own2, twin0, twin1, twin2, near0, near1, near2, far0]
    early = pl.pallas_call(
        functools.partial(early_kernel, n_place, k_half),
        in_specs=[scalars] * 3 + [here] * len(operands),
        out_specs=here,
        out_shape=terms,
        compiler_params=params,
        cost_estimate=cost,
    )(k_irrep, i_irrep, virt_count, *operands)
    far123, early, *own3 = hold(far123, early, *own3)
    own3 = jnp.concatenate(own3)
    twin3 = flip(own3, 1)
    operands = [own1, own2, own3, twin1, twin2, twin3, near3, far123, early]
    tile, _ = pl.pallas_call(
        functools.partial(late_kernel, n_place, k_half),
        in_specs=[scalars] * 4 + [here] * len(operands),
        out_specs=[here, here],
        out_shape=[jax.ShapeDtypeStruct((n_grp, 2, j_count, slab, width), jnp.bfloat16), terms],
        input_output_aliases={3 + len(operands): 1},
        compiler_params=params,
        cost_estimate=cost,
    )(k_irrep, i_irrep, virt_count, j_irrep, *operands)
    result = lax.all_to_all(tile, "grp", split_axis=0, concat_axis=0, tiled=True)
    result = result.reshape(2, i_total, j_count, slab, width)
    return result[0] + result[1]


def shards(n_batch, n_grp, amps, cycle_inter, k_irrep, i_irrep, j_irrep, virt_count):
    operands = (amps, cycle_inter, k_irrep, i_irrep, j_irrep, virt_count)
    n_irrep = virt_count.shape[0]
    if n_batch == 2 and n_grp == 2 * n_irrep and n_irrep == 8 and amps.shape[1] == n_grp:
        return shards_tiled(*operands)
    return shards_any(n_batch, n_grp, *operands)


def solution(mesh):
    return jax.shard_map(
        functools.partial(shards, mesh.shape["batch"], mesh.shape["grp"]),
        mesh=mesh,
        in_specs=(P("batch", None, "grp", None), P("batch", "grp", None, None), P(), P(), P(), P()),
        out_specs=P(None, "batch", "grp", None),
        check_vma=False,
    )
```

```python
import functools

import jax
import jax.numpy as jnp
from jax import lax
from jax.experimental import pallas as pl
from jax.experimental.pallas import tpu as pltpu
from jax.sharding import PartitionSpec as P


def contract_kernel(n_k, width, labels_ref, *refs):
    amp_refs = refs[:n_k]
    inter_refs = refs[n_k:2 * n_k]
    out_ref = refs[2 * n_k]
    p = pl.program_id(0)
    n_irrep = pl.num_programs(0)
    j_count = out_ref.shape[1]
    i_label = labels_ref[n_k]
    j_first = n_k + 1
    count_first = j_first + j_count
    row = lax.broadcasted_iota(jnp.int32, (width, width), 0)
    col = lax.broadcasted_iota(jnp.int32, (width, width), 1)
    acc = None
    for k in range(n_k):
        c_count = labels_ref[count_first + (labels_ref[k] ^ i_label ^ p)]
        amp = amp_refs[k][...].reshape(width, width)
        amp = jnp.where(row < c_count, amp, jnp.zeros((), amp.dtype))
        inter = inter_refs[k][...].reshape(width, j_count * width)
        term = lax.dot_general(amp, inter, (((0,), (0,)), ((), ())), preferred_element_type=jnp.float32)
        acc = term if acc is None else acc + term
    a_count = labels_ref[count_first + p]
    parts, rows = out_ref.shape[0], out_ref.shape[2]
    for j in range(j_count):
        b_count = labels_ref[count_first + (p ^ i_label ^ labels_ref[j_first + j])]
        live = (row < a_count) & (col < b_count)
        block = jnp.where(live, acc[:, j * width:(j + 1) * width], 0.0).astype(out_ref.dtype)
        out_ref[:, j] = block.reshape(parts, rows, width)


def contract(labels, amps, inter, n_irrep, j_count):
    devices, _, slab, width = amps[0].shape
    parts = devices // n_irrep
    n_k = sum(x.shape[1] for x in amps)

    def block_of(k, at):
        def index(p, labels):
            return (labels[k] ^ labels[n_k] ^ p, at, 0, 0)
        return index

    amp_ops, amp_specs, inter_specs = [], [], []
    for a in amps:
        for at in range(a.shape[1]):
            amp_specs.append(pl.BlockSpec((parts, 1, slab, width), block_of(len(amp_ops), at)))
            amp_ops.append(a)
    for k in range(n_k):
        inter_specs.append(pl.BlockSpec((parts, 1, slab, j_count * width), block_of(k, k)))
    flops = 2 * n_k * n_irrep * width ** 3 * j_count
    return pl.pallas_call(
        functools.partial(contract_kernel, n_k, width),
        grid_spec=pltpu.PrefetchScalarGridSpec(
            num_scalar_prefetch=1,
            grid=(n_irrep,),
            in_specs=amp_specs + inter_specs,
            out_specs=pl.BlockSpec((parts, j_count, slab, width), lambda p, labels: (p, 0, 0, 0)),
        ),
        out_shape=jax.ShapeDtypeStruct((devices, j_count, slab, width), jnp.bfloat16),
        compiler_params=pltpu.CompilerParams(vmem_limit_bytes=48 * 2 ** 20),
        cost_estimate=pl.CostEstimate(flops=flops, bytes_accessed=flops // 128, transcendentals=0),
    )(labels, *amp_ops, *([inter] * n_k))


def shards_any(n_batch, n_grp, amps, cycle_inter, k_irrep, i_irrep, j_irrep, virt_count):
    k_local, i_total, slab, width = amps.shape
    n_irrep = virt_count.shape[0]
    j_total = cycle_inter.shape[2]
    j_count = j_total // n_batch
    me_b = lax.axis_index("batch")
    me_g = lax.axis_index("grp")
    i_count = i_total // n_grp

    split = cycle_inter.reshape(k_local, slab, n_batch, j_count * width)
    if n_batch == 2:
        swap = [(0, 1), (1, 0)]
        own = lax.dynamic_index_in_dim(split, me_b, 2, keepdims=False)
        away = lax.dynamic_index_in_dim(split, 1 - me_b, 2, keepdims=False)
        mine = jnp.concatenate([own, lax.ppermute(away, "batch", swap)])
        k_labels = jnp.concatenate([
            lax.dynamic_slice_in_dim(k_irrep, me_b * k_local, k_local),
            lax.dynamic_slice_in_dim(k_irrep, (1 - me_b) * k_local, k_local),
        ])
    else:
        mine = lax.all_to_all(split.transpose(2, 0, 1, 3), "batch", split_axis=0, concat_axis=0, tiled=True)
        mine = mine.reshape(n_batch * k_local, slab, j_count * width)
        k_labels = k_irrep
    inter_all = lax.all_gather(mine, "grp", axis=0, tiled=False)

    sends = amps.transpose(1, 0, 2, 3).reshape(n_grp, i_count, k_local, slab, width)
    got = lax.all_to_all(sends, "grp", split_axis=0, concat_axis=0, tiled=True)
    if n_batch == 2:
        amp_parts = [got, lax.ppermute(got, "batch", swap)]
    else:
        gathered = lax.all_gather(got, "batch", axis=0, tiled=False)
        amp_parts = [gathered[b] for b in range(n_batch)]

    j_labels = lax.dynamic_slice_in_dim(j_irrep, me_b * j_count, j_count)
    outs = []
    for i in range(i_count):
        i_label = lax.dynamic_slice_in_dim(i_irrep, me_g * i_count + i, 1)
        labels = jnp.concatenate([k_labels, i_label, j_labels, virt_count])
        outs.append(contract(labels, [a[:, i] for a in amp_parts], inter_all, n_irrep, j_count))
    partial = outs[0][:, None] if i_count == 1 else jnp.stack(outs, axis=1)
    result = lax.all_to_all(partial, "grp", split_axis=0, concat_axis=0, tiled=True)
    return result.reshape(i_total, j_count, slab, width)


def device_labels(n_place, k_half, k_irrep, i_irrep):
    me_b, me_g = lax.axis_index("batch"), lax.axis_index("grp")
    i_labels = [i_irrep[2 * (me_g % (2 * n_place)) + i] for i in range(2)]
    k_labels = [k_irrep[(me_b ^ half) * k_half + k] for half in range(2) for k in range(k_half)]
    return me_b, me_g % 2, me_g // 2, k_labels, i_labels


def add_terms(n_place, k_half, pieces, k_irrep, i_irrep, virt_count, total):
    width = total.shape[2]
    _, core, first_c, k_labels, i_labels = device_labels(n_place, k_half, k_irrep, i_irrep)
    row = lax.broadcasted_iota(jnp.int32, (width, width), 0)
    slot = (row + core * (width // 2)) & (width - 1)
    for at, half, side, own, twin in pieces:
        c = first_c ^ at
        live = slot < virt_count[c]
        for k in range(k_half):
            amps = []
            for i in range(2):
                amp = side[:, k, i].reshape(width, width)
                amps.append(jnp.where(live, amp, jnp.zeros((), amp.dtype)))
            inter = jnp.concatenate([own[k], twin[k]], axis=0)
            term = lax.dot_general(
                jnp.concatenate(amps, axis=1), inter, (((0,), (0,)), ((), ())), preferred_element_type=jnp.float32
            )
            for i in range(2):
                p = c ^ k_labels[half * k_half + k] ^ i_labels[i]
                total[i, p] += term[i * width:(i + 1) * width]


def early_kernel(n_place, k_half, k_irrep, i_irrep, virt_count, *refs):
    m = n_place - 1
    own, twin, near, (far, total) = refs[:m], refs[m:2 * m], refs[2 * m:3 * m], refs[3 * m:]
    total[...] = jnp.zeros_like(total)
    pieces = [(at, 0, near[at], own[at], twin[at]) for at in range(m)]
    pieces.append((0, 1, far, own[0].at[pl.ds(k_half, k_half)], twin[0].at[pl.ds(k_half, k_half)]))
    add_terms(n_place, k_half, pieces, k_irrep, i_irrep, virt_count, total)


def late_kernel(n_place, k_half, k_irrep, i_irrep, virt_count, j_irrep, *refs):
    m = n_place - 1
    own, twin, (near, far, _, out_ref, total) = refs[:m + 1], refs[m + 1:2 * m + 2], refs[2 * m + 2:]
    n_irrep, width = total.shape[1:3]
    j_count = out_ref.shape[2]
    later = pl.ds(k_half, k_half)
    pieces = [(at, 1, far.at[at - 1], own[at - 1].at[later], twin[at - 1].at[later]) for at in range(1, m)]
    pieces += [(m, 0, near, own[m - 1], twin[m - 1]), (m, 1, far.at[m - 1], own[m], twin[m])]
    add_terms(n_place, k_half, pieces, k_irrep, i_irrep, virt_count, total)
    me_b, _, _, _, i_labels = device_labels(n_place, k_half, k_irrep, i_irrep)
    row = lax.broadcasted_iota(jnp.int32, (width, width), 0)
    col = lax.broadcasted_iota(jnp.int32, (width, width), 1)

    @pl.loop(0, n_irrep)
    def _(p):
        a_live = row < virt_count[p]
        for i in range(2):
            for j in range(j_count):
                b = p ^ i_labels[i] ^ j_irrep[me_b * j_count + j]
                live = a_live & (col < virt_count[b])
                block = jnp.where(live, total[i, p, :, j * width:(j + 1) * width], 0.0).astype(out_ref.dtype)
                for side in range(2):
                    out_ref[2 * p + side, i, j] = block[side * width // 2:(side + 1) * width // 2]


def shards_tiled(amps, cycle_inter, k_irrep, i_irrep, j_irrep, virt_count):
    k_half, i_total, slab, width = amps.shape
    n_irrep = virt_count.shape[0]
    j_count = cycle_inter.shape[2] // 2
    n_place = n_irrep // 2
    n_grp = 4 * n_place
    me_b = lax.axis_index("batch")
    me_g = lax.axis_index("grp")
    core, place = me_g % 2, (me_g // 2) % n_place
    swap = [(0, 1), (1, 0)]

    def flip(x, bits):
        return lax.ppermute(x, "grp", [(d, d ^ bits) for d in range(n_grp)])

    def hold(*xs):
        return lax.optimization_barrier(xs)

    def over(x):
        return lax.ppermute(x, "batch", swap)

    low, high = cycle_inter[:, :, :j_count], cycle_inter[:, :, j_count:]
    mine = jnp.where(me_b == 0, low, high).reshape(k_half, slab, j_count * width)
    away = jnp.where(me_b == 0, high, low).reshape(k_half, slab, j_count * width)
    parts = amps.reshape(k_half, n_place, 2, 2, slab, width)
    keep = lax.dynamic_index_in_dim(parts, core, 2, keepdims=False)
    take = flip(lax.dynamic_index_in_dim(parts, 1 - core, 2, keepdims=False), 1)
    i_parts = jnp.stack([keep, take])

    def i_part(at):
        return lax.dynamic_index_in_dim(i_parts, at, 2, keepdims=False)

    other = over(away)
    near0, near1, near2, near3 = i_part(place), *(flip(i_part(place ^ m), 2 * m) for m in range(1, n_place))
    far0 = over(near0)
    near1, near2, near3, far0 = hold(near1, near2, near3, far0)
    own0 = jnp.concatenate([mine, other])
    own1, own2, twin0 = flip(own0, 2), flip(own0, 4), flip(own0, 1)
    far123 = over(jnp.stack([near1, near2, near3]))
    own1, own2, twin0 = hold(own1, own2, twin0)
    own3 = flip(own1[:k_half], 4), flip(own2[k_half:], 2)
    twin1, twin2 = flip(own1, 1), flip(own2, 1)
    here, scalars = pl.BlockSpec(memory_space=pltpu.VMEM), pl.BlockSpec(memory_space=pltpu.SMEM)
    terms = jax.ShapeDtypeStruct((2, n_irrep, width, j_count * width), jnp.float32)
    flops = 2 * k_half * 2 * n_place * width ** 3 * j_count
    cost = pl.CostEstimate(flops=flops, bytes_accessed=2 ** 20, transcendentals=0)
    params = pltpu.CompilerParams(vmem_limit_bytes=16 * 2 ** 20)
    operands = [own0, own1, own2, twin0, twin1, twin2, near0, near1, near2, far0]
    early = pl.pallas_call(
        functools.partial(early_kernel, n_place, k_half),
        in_specs=[scalars] * 3 + [here] * len(operands),
        out_specs=here,
        out_shape=terms,
        compiler_params=params,
        cost_estimate=cost,
    )(k_irrep, i_irrep, virt_count, *operands)
    far123, early, *own3 = hold(far123, early, *own3)
    twin3 = [flip(x, 1) for x in own3]
    operands = [own1, own2, *own3, twin1, twin2, *twin3, near3, far123, early]
    tile, _ = pl.pallas_call(
        functools.partial(late_kernel, n_place, k_half),
        in_specs=[scalars] * 4 + [here] * len(operands),
        out_specs=[here, here],
        out_shape=[jax.ShapeDtypeStruct((n_grp, 2, j_count, slab, width), jnp.bfloat16), terms],
        input_output_aliases={3 + len(operands): 1},
        compiler_params=params,
        cost_estimate=cost,
    )(k_irrep, i_irrep, virt_count, j_irrep, *operands)
    result = lax.all_to_all(tile, "grp", split_axis=0, concat_axis=0, tiled=True)
    result = result.reshape(2, i_total, j_count, slab, width)
    return result[0] + result[1]


def shards(n_batch, n_grp, amps, cycle_inter, k_irrep, i_irrep, j_irrep, virt_count):
    operands = (amps, cycle_inter, k_irrep, i_irrep, j_irrep, virt_count)
    n_irrep = virt_count.shape[0]
    if n_batch == 2 and n_grp == 2 * n_irrep and n_irrep == 8 and amps.shape[1] == n_grp:
        return shards_tiled(*operands)
    return shards_any(n_batch, n_grp, *operands)


def solution(mesh):
    return jax.shard_map(
        functools.partial(shards, mesh.shape["batch"], mesh.shape["grp"]),
        mesh=mesh,
        in_specs=(P("batch", None, "grp", None), P("batch", "grp", None, None), P(), P(), P(), P()),
        out_specs=P(None, "batch", "grp", None),
        check_vma=False,
    )
```

```python
import functools

import jax
import jax.numpy as jnp
from jax import lax
from jax.experimental import pallas as pl
from jax.experimental.pallas import tpu as pltpu
from jax.sharding import PartitionSpec as P


def contract_kernel(n_k, width, labels_ref, *refs):
    amp_refs = refs[:n_k]
    inter_refs = refs[n_k:2 * n_k]
    out_ref = refs[2 * n_k]
    p = pl.program_id(0)
    n_irrep = pl.num_programs(0)
    j_count = out_ref.shape[1]
    i_label = labels_ref[n_k]
    j_first = n_k + 1
    count_first = j_first + j_count
    row = lax.broadcasted_iota(jnp.int32, (width, width), 0)
    col = lax.broadcasted_iota(jnp.int32, (width, width), 1)
    acc = None
    for k in range(n_k):
        c_count = labels_ref[count_first + (labels_ref[k] ^ i_label ^ p)]
        amp = amp_refs[k][...].reshape(width, width)
        amp = jnp.where(row < c_count, amp, jnp.zeros((), amp.dtype))
        inter = inter_refs[k][...].reshape(width, j_count * width)
        term = lax.dot_general(amp, inter, (((0,), (0,)), ((), ())), preferred_element_type=jnp.float32)
        acc = term if acc is None else acc + term
    a_count = labels_ref[count_first + p]
    parts, rows = out_ref.shape[0], out_ref.shape[2]
    for j in range(j_count):
        b_count = labels_ref[count_first + (p ^ i_label ^ labels_ref[j_first + j])]
        live = (row < a_count) & (col < b_count)
        block = jnp.where(live, acc[:, j * width:(j + 1) * width], 0.0).astype(out_ref.dtype)
        out_ref[:, j] = block.reshape(parts, rows, width)


def contract(labels, amps, inter, n_irrep, j_count):
    devices, _, slab, width = amps[0].shape
    parts = devices // n_irrep
    n_k = sum(x.shape[1] for x in amps)

    def block_of(k, at):
        def index(p, labels):
            return (labels[k] ^ labels[n_k] ^ p, at, 0, 0)
        return index

    amp_ops, amp_specs, inter_specs = [], [], []
    for a in amps:
        for at in range(a.shape[1]):
            amp_specs.append(pl.BlockSpec((parts, 1, slab, width), block_of(len(amp_ops), at)))
            amp_ops.append(a)
    for k in range(n_k):
        inter_specs.append(pl.BlockSpec((parts, 1, slab, j_count * width), block_of(k, k)))
    flops = 2 * n_k * n_irrep * width ** 3 * j_count
    return pl.pallas_call(
        functools.partial(contract_kernel, n_k, width),
        grid_spec=pltpu.PrefetchScalarGridSpec(
            num_scalar_prefetch=1,
            grid=(n_irrep,),
            in_specs=amp_specs + inter_specs,
            out_specs=pl.BlockSpec((parts, j_count, slab, width), lambda p, labels: (p, 0, 0, 0)),
        ),
        out_shape=jax.ShapeDtypeStruct((devices, j_count, slab, width), jnp.bfloat16),
        compiler_params=pltpu.CompilerParams(vmem_limit_bytes=48 * 2 ** 20),
        cost_estimate=pl.CostEstimate(flops=flops, bytes_accessed=flops // 128, transcendentals=0),
    )(labels, *amp_ops, *([inter] * n_k))


def shards_any(n_batch, n_grp, amps, cycle_inter, k_irrep, i_irrep, j_irrep, virt_count):
    k_local, i_total, slab, width = amps.shape
    n_irrep = virt_count.shape[0]
    j_total = cycle_inter.shape[2]
    j_count = j_total // n_batch
    me_b = lax.axis_index("batch")
    me_g = lax.axis_index("grp")
    i_count = i_total // n_grp

    split = cycle_inter.reshape(k_local, slab, n_batch, j_count * width)
    if n_batch == 2:
        swap = [(0, 1), (1, 0)]
        own = lax.dynamic_index_in_dim(split, me_b, 2, keepdims=False)
        away = lax.dynamic_index_in_dim(split, 1 - me_b, 2, keepdims=False)
        mine = jnp.concatenate([own, lax.ppermute(away, "batch", swap)])
        k_labels = jnp.concatenate([
            lax.dynamic_slice_in_dim(k_irrep, me_b * k_local, k_local),
            lax.dynamic_slice_in_dim(k_irrep, (1 - me_b) * k_local, k_local),
        ])
    else:
        mine = lax.all_to_all(split.transpose(2, 0, 1, 3), "batch", split_axis=0, concat_axis=0, tiled=True)
        mine = mine.reshape(n_batch * k_local, slab, j_count * width)
        k_labels = k_irrep
    inter_all = lax.all_gather(mine, "grp", axis=0, tiled=False)

    sends = amps.transpose(1, 0, 2, 3).reshape(n_grp, i_count, k_local, slab, width)
    got = lax.all_to_all(sends, "grp", split_axis=0, concat_axis=0, tiled=True)
    if n_batch == 2:
        amp_parts = [got, lax.ppermute(got, "batch", swap)]
    else:
        gathered = lax.all_gather(got, "batch", axis=0, tiled=False)
        amp_parts = [gathered[b] for b in range(n_batch)]

    j_labels = lax.dynamic_slice_in_dim(j_irrep, me_b * j_count, j_count)
    outs = []
    for i in range(i_count):
        i_label = lax.dynamic_slice_in_dim(i_irrep, me_g * i_count + i, 1)
        labels = jnp.concatenate([k_labels, i_label, j_labels, virt_count])
        outs.append(contract(labels, [a[:, i] for a in amp_parts], inter_all, n_irrep, j_count))
    partial = outs[0][:, None] if i_count == 1 else jnp.stack(outs, axis=1)
    result = lax.all_to_all(partial, "grp", split_axis=0, concat_axis=0, tiled=True)
    return result.reshape(i_total, j_count, slab, width)


def device_labels(n_place, k_half, k_irrep, i_irrep):
    me_b, me_g = lax.axis_index("batch"), lax.axis_index("grp")
    i_labels = [i_irrep[2 * (me_g % (2 * n_place)) + i] for i in range(2)]
    k_labels = [k_irrep[(me_b ^ half) * k_half + k] for half in range(2) for k in range(k_half)]
    return me_b, me_g % 2, me_g // 2, k_labels, i_labels


def add_terms(n_place, k_half, pieces, k_irrep, i_irrep, virt_count, total):
    width = total.shape[2]
    _, core, first_c, k_labels, i_labels = device_labels(n_place, k_half, k_irrep, i_irrep)
    row = lax.broadcasted_iota(jnp.int32, (width, width), 0)
    slot = (row + core * (width // 2)) & (width - 1)
    for at, half, side, own, twin in pieces:
        c = first_c ^ at
        live = slot < virt_count[c]
        for k in range(k_half):
            amps = []
            for i in range(2):
                amp = side[:, k, i].reshape(width, width)
                amps.append(jnp.where(live, amp, jnp.zeros((), amp.dtype)))
            inter = jnp.concatenate([own[k], twin[k]], axis=0)
            term = lax.dot_general(
                jnp.concatenate(amps, axis=1), inter, (((0,), (0,)), ((), ())), preferred_element_type=jnp.float32
            )
            for i in range(2):
                p = c ^ k_labels[half * k_half + k] ^ i_labels[i]
                total[i, p] += term[i * width:(i + 1) * width]


def early_kernel(n_place, k_half, k_irrep, i_irrep, virt_count, *refs):
    m = n_place - 1
    own, twin, near, (far, total) = refs[:m], refs[m:2 * m], refs[2 * m:3 * m], refs[3 * m:]
    total[...] = jnp.zeros_like(total)
    pieces = [(at, 0, near[at], own[at], twin[at]) for at in range(m)]
    pieces.append((0, 1, far, own[0].at[pl.ds(k_half, k_half)], twin[0].at[pl.ds(k_half, k_half)]))
    add_terms(n_place, k_half, pieces, k_irrep, i_irrep, virt_count, total)


def late_kernel(n_place, k_half, k_irrep, i_irrep, virt_count, j_irrep, *refs):
    m = n_place - 1
    own, twin, (near, far, _, out_ref, total) = refs[:m + 1], refs[m + 1:2 * m + 2], refs[2 * m + 2:]
    n_irrep, width = total.shape[1:3]
    j_count = out_ref.shape[2]
    later = pl.ds(k_half, k_half)
    pieces = [(at, 1, far.at[at - 1], own[at - 1].at[later], twin[at - 1].at[later]) for at in range(1, m)]
    pieces += [(m, 0, near, own[m - 1], twin[m - 1]), (m, 1, far.at[m - 1], own[m], twin[m])]
    add_terms(n_place, k_half, pieces, k_irrep, i_irrep, virt_count, total)
    me_b, _, _, _, i_labels = device_labels(n_place, k_half, k_irrep, i_irrep)
    row = lax.broadcasted_iota(jnp.int32, (width, width), 0)
    col = lax.broadcasted_iota(jnp.int32, (width, width), 1)

    @pl.loop(0, n_irrep)
    def _(p):
        a_live = row < virt_count[p]
        for i in range(2):
            for j in range(j_count):
                b = p ^ i_labels[i] ^ j_irrep[me_b * j_count + j]
                live = a_live & (col < virt_count[b])
                block = jnp.where(live, total[i, p, :, j * width:(j + 1) * width], 0.0).astype(out_ref.dtype)
                for side in range(2):
                    out_ref[2 * p + side, i, j] = block[side * width // 2:(side + 1) * width // 2]


def shards_tiled(amps, cycle_inter, k_irrep, i_irrep, j_irrep, virt_count):
    k_half, i_total, slab, width = amps.shape
    n_irrep = virt_count.shape[0]
    j_count = cycle_inter.shape[2] // 2
    n_place = n_irrep // 2
    n_grp = 4 * n_place
    me_b = lax.axis_index("batch")
    me_g = lax.axis_index("grp")
    core, place = me_g % 2, (me_g // 2) % n_place
    swap = [(0, 1), (1, 0)]

    def flip(x, bits):
        return lax.ppermute(x, "grp", [(d, d ^ bits) for d in range(n_grp)])

    def hold(*xs):
        return lax.optimization_barrier(xs)

    def over(x):
        return lax.ppermute(x, "batch", swap)

    low, high = cycle_inter[:, :, :j_count], cycle_inter[:, :, j_count:]
    mine = jnp.where(me_b == 0, low, high).reshape(k_half, slab, j_count * width)
    away = jnp.where(me_b == 0, high, low).reshape(k_half, slab, j_count * width)
    parts = amps.reshape(k_half, n_place, 2, 2, slab, width)
    take = flip(lax.dynamic_index_in_dim(parts, 1 - core, 2, keepdims=False), 1)
    parts, away = hold(parts, away)
    keep = lax.dynamic_index_in_dim(parts, core, 2, keepdims=False)
    i_parts = jnp.stack([keep, take])

    def i_part(at):
        return lax.dynamic_index_in_dim(i_parts, at, 2, keepdims=False)

    other = over(away)
    near0, near1, near2, near3 = i_part(place), *(flip(i_part(place ^ m), 2 * m) for m in range(1, n_place))
    far0 = over(near0)
    near1, near2, near3, far0 = hold(near1, near2, near3, far0)
    own0 = jnp.concatenate([mine, other])
    own1, own2, twin0 = flip(own0, 2), flip(own0, 4), flip(own0, 1)
    far123 = over(jnp.stack([near1, near2, near3]))
    own1, own2, twin0 = hold(own1, own2, twin0)
    own3 = flip(own1[:k_half], 4), flip(own2[k_half:], 2)
    twin1, twin2 = flip(own1, 1), flip(own2, 1)
    here, scalars = pl.BlockSpec(memory_space=pltpu.VMEM), pl.BlockSpec(memory_space=pltpu.SMEM)
    terms = jax.ShapeDtypeStruct((2, n_irrep, width, j_count * width), jnp.float32)
    flops = 2 * k_half * 2 * n_place * width ** 3 * j_count
    cost = pl.CostEstimate(flops=flops, bytes_accessed=2 ** 20, transcendentals=0)
    params = pltpu.CompilerParams(vmem_limit_bytes=16 * 2 ** 20)
    operands = [own0, own1, own2, twin0, twin1, twin2, near0, near1, near2, far0]
    early = pl.pallas_call(
        functools.partial(early_kernel, n_place, k_half),
        in_specs=[scalars] * 3 + [here] * len(operands),
        out_specs=here,
        out_shape=terms,
        compiler_params=params,
        cost_estimate=cost,
    )(k_irrep, i_irrep, virt_count, *operands)
    far123, early, *own3 = hold(far123, early, *own3)
    twin3 = [flip(x, 1) for x in own3]
    operands = [own1, own2, *own3, twin1, twin2, *twin3, near3, far123, early]
    tile, _ = pl.pallas_call(
        functools.partial(late_kernel, n_place, k_half),
        in_specs=[scalars] * 4 + [here] * len(operands),
        out_specs=[here, here],
        out_shape=[jax.ShapeDtypeStruct((n_grp, 2, j_count, slab, width), jnp.bfloat16), terms],
        input_output_aliases={3 + len(operands): 1},
        compiler_params=params,
        cost_estimate=cost,
    )(k_irrep, i_irrep, virt_count, j_irrep, *operands)
    result = lax.all_to_all(tile, "grp", split_axis=0, concat_axis=0, tiled=True)
    result = result.reshape(2, i_total, j_count, slab, width)
    return result[0] + result[1]


def shards(n_batch, n_grp, amps, cycle_inter, k_irrep, i_irrep, j_irrep, virt_count):
    operands = (amps, cycle_inter, k_irrep, i_irrep, j_irrep, virt_count)
    n_irrep = virt_count.shape[0]
    if n_batch == 2 and n_grp == 2 * n_irrep and n_irrep == 8 and amps.shape[1] == n_grp:
        return shards_tiled(*operands)
    return shards_any(n_batch, n_grp, *operands)


def solution(mesh):
    return jax.shard_map(
        functools.partial(shards, mesh.shape["batch"], mesh.shape["grp"]),
        mesh=mesh,
        in_specs=(P("batch", None, "grp", None), P("batch", "grp", None, None), P(), P(), P(), P()),
        out_specs=P(None, "batch", "grp", None),
        check_vma=False,
    )
```
